32 devices in a mesh: grp: 2 (over x), gx: 16 (over z, y, core).
Axes of the slice: x: 2, y: 2, z: 4, core: 2. Of those that a mesh axis runs over, the one named last changes fastest.
Arguments:
- velocity: float32 [6, 256, 64, 128], P('grp', 'gx'), parts along dimension 0, may hold values from -6 to 6
- vfrac_class: int32 [512, 64, 128], P(('grp', 'gx')), parts along dimension 0, may hold values from 0 to 3
- cut_cells: int32 [32768], P(('grp', 'gx')), parts along dimension 0, may hold values from 1 to 131070, as said below
- cut_count: int32 [32], P(('grp', 'gx')), parts along dimension 0, may hold values from 128 to 1024, as said below
- offsets: int32 [18, 16384], P('grp', 'gx'), parts along dimension 0, may hold values from 0 to 26, as said below
Outputs:
- projected: float32 [6, 256, 64, 128], P('grp', 'gx'), parts along dimension 0
- potential: float32 [512, 64, 128], P(('grp', 'gx')), parts along dimension 0
The draws below stay inside these ranges and needn't reach their ends.
There are 2 independent parts, one for each index of `grp`. The reference program is written for one: setup_inputs(seed, part) draws one part's arguments, and reference() takes and returns one part's arrays. A program takes and returns all parts, laid end to end along the dimension named above; each array names one. Nothing has to cross between parts.
Inputs may be any that keep to these rules, and one draw needn't show every extreme that they name: `cut_cells`: each device's block of 1024 entries holds distinct local cell numbers x * 64 * 128 + y * 128 + z of that device's cells, with z from 1 to 126; in every group of four slots the first cell has x = 0, the second x = 15, the other two x from 1 to 14. `cut_count`: some devices have all 1024 slots live, most have fewer. `offsets`: code (dx + 1) * 9 + (dy + 1) * 3 + (dz + 1) of a cell of the 3 x 3 x 3 block around the cut cell; entry 0 is 13, the cut cell itself; entries 1 and 2 have dx = -1, entries 3 and 4 have dx = 1, the others dx = 0; the 9 codes of one slot are distinct.
All inputs are finite; a program needn't handle non-finite values. Where the reference program divides by a largest or mean magnitude, that divisor is 1e-20 or more.
Results may differ from the reference program's by a relative error of at most 0.0003.
Values sent between devices are 32-bit elements; how exact they have to be, the bound alone decides.
A program may use at most 320 MiB of HBM per device.

```python
import jax
import jax.numpy as jnp
from jax import lax

CX = 16
NY = 64
NZ = 128
CUT_DEV = 1024
HOOD = 9
LEVELS = 3
CYCLES = 2
SWEEPS = 2
COARSE = 4
NX = 256
CELLS_CUT = 16384
N_GX = 16


def draw_velocity(key, part):
    key = jax.random.fold_in(key, 11)
    base_key, place_key, size_key, sign_key = jax.random.split(key, 4)
    along = jnp.arange(NX, dtype=jnp.float32) / max(NX - 1, 1)
    profile = (0.5 + jnp.abs(2.0 * along - 1.0))[None, :, None, None]
    raw = jnp.clip(jax.random.normal(base_key, (3, NX, NY, NZ), jnp.float32), -3.0, 3.0)
    field = (raw * profile).reshape(-1)
    total = 3 * NX * NY * NZ
    spot = jax.random.randint(place_key, (), 0, total)
    magnitude = jax.random.uniform(size_key, (), jnp.float32, 4.6, 6.0)
    sign = jnp.where(jax.random.bernoulli(sign_key), 1.0, -1.0).astype(jnp.float32)
    field = jnp.where(jnp.arange(total, dtype=jnp.int32) == spot, sign * magnitude, field)
    return field.reshape(3, NX, NY, NZ).astype(jnp.float32)


def draw_cut_cells(key, part):
    key = jax.random.fold_in(key, 12)
    device_keys = jax.random.split(key, N_GX)
    quarter = CUT_DEV // 4
    column_cells = NY * (NZ - 2)

    def layer_cells(pick, x_value):
        return (x_value * NY + pick // (NZ - 2)) * NZ + pick % (NZ - 2) + 1

    def one_device(sub_key):
        lower_key, upper_key, inner_key = jax.random.split(sub_key, 3)
        lower_cells = layer_cells(jax.random.permutation(lower_key, column_cells)[:quarter], 0)
        upper_cells = layer_cells(jax.random.permutation(upper_key, column_cells)[:quarter], CX - 1)
        inner_pick = jax.random.permutation(inner_key, (CX - 2) * column_cells)[:2 * quarter]
        inner_x = inner_pick // column_cells + 1
        inner_rest = inner_pick % column_cells
        inner_cells = (inner_x * NY + inner_rest // (NZ - 2)) * NZ + inner_rest % (NZ - 2) + 1
        return jnp.stack([lower_cells, upper_cells, inner_cells[:quarter], inner_cells[quarter:]], axis=1).reshape(-1)
    return jax.vmap(one_device)(device_keys).reshape(-1).astype(jnp.int32)


def draw_cut_count(key, part):
    key = jax.random.fold_in(key, 13)
    first_key, second_key = jax.random.split(key)
    band_size = max(1, N_GX // 4)
    start_rank = jax.random.randint(first_key, (), 0, N_GX)
    ranks = jnp.arange(N_GX)
    inside = (ranks - start_rank) % N_GX < band_size
    sparse = jax.random.randint(second_key, (N_GX,), max(8, CUT_DEV // 8), CUT_DEV // 2 + 1)
    return jnp.where(inside, CUT_DEV, sparse).astype(jnp.int32)


def draw_offsets(key, part):
    key = jax.random.fold_in(key, 14)
    slot_keys = jax.random.split(key, CELLS_CUT)

    def pick_codes(row_key):
        low_key, high_key, mid_key = jax.random.split(row_key, 3)
        low = jax.random.permutation(low_key, 9)[:2]
        high = jax.random.permutation(high_key, 9)[:2] + 18
        mid = jax.random.permutation(mid_key, 8)[:HOOD - 5]
        mid = mid + 9 + (mid >= 4).astype(mid.dtype)
        return jnp.concatenate([low, high, mid])
    codes = jax.vmap(pick_codes)(slot_keys)
    selfish = jnp.full((1, CELLS_CUT), 13, dtype=codes.dtype)
    return jnp.concatenate([selfish, codes.T], axis=0).astype(jnp.int32)


def plant(result, key, least, largest):
    longest = result.shape.index(max(result.shape))
    spots = []
    for shift in (0, 1):
        where = [jax.random.randint(jax.random.fold_in(key, axis), (), 0, length) for axis, length in enumerate(result.shape)]
        where[longest] = (where[longest] + shift) % result.shape[longest]
        spots.append(tuple(where))
    return result.at[spots[0]].set(least).at[spots[1]].set(largest)


def setup_inputs(seed: int = 0, part: int = 0) -> dict:
    key_list = jax.random.split(jax.random.key(seed), 6)
    part_splits = jax.random.split(jax.random.fold_in(key_list[5], part), 6)
    return {
        "velocity": draw_velocity(jax.random.fold_in(jax.random.fold_in(key_list[5], part), 71), part),
        "vfrac_class": plant(jax.random.randint(part_splits[1], (NX, NY, NZ), 0, 4), jax.random.fold_in(part_splits[1], 1), 0, 3).astype(jnp.int32),
        "cut_cells": draw_cut_cells(jax.random.fold_in(jax.random.fold_in(key_list[5], part), 71), part),
        "cut_count": draw_cut_count(jax.random.fold_in(jax.random.fold_in(key_list[5], part), 71), part),
        "offsets": draw_offsets(jax.random.fold_in(jax.random.fold_in(key_list[5], part), 71), part),
    }


courant = 0.5
damping = 0.8


def minmod_limit(first_diff, second_diff):
    return 0.5 * (jnp.sign(first_diff) + jnp.sign(second_diff)) * jnp.minimum(jnp.abs(first_diff), jnp.abs(second_diff))


def take_span(array, begin, finish, direction):
    return lax.slice_in_dim(array, begin, finish, axis=direction)


def face_balance(state_pad, speed_pad, fraction_pad, direction, walled):
    cell_count = state_pad.shape[direction] - 4
    middle = take_span(state_pad, 1, cell_count + 3, direction)
    slopes = minmod_limit(middle - take_span(state_pad, 0, cell_count + 2, direction), take_span(state_pad, 2, cell_count + 4, direction) - middle)
    left_side = take_span(middle + 0.5 * slopes, 0, cell_count + 1, direction)
    right_side = take_span(middle - 0.5 * slopes, 1, cell_count + 2, direction)
    speed_mid = take_span(speed_pad, 1, cell_count + 3, direction)
    fraction_mid = take_span(fraction_pad, 1, cell_count + 3, direction)
    face_speed = 0.5 * (take_span(speed_mid, 0, cell_count + 1, direction) + take_span(speed_mid, 1, cell_count + 2, direction))
    aperture = jnp.minimum(take_span(fraction_mid, 0, cell_count + 1, direction), take_span(fraction_mid, 1, cell_count + 2, direction))
    fluxes = aperture * face_speed * jnp.where(face_speed > 0, left_side, right_side)
    if walled:
        edge_zero = jnp.zeros_like(take_span(fluxes, 0, 1, direction))
        fluxes = jnp.concatenate([edge_zero, take_span(fluxes, 1, cell_count, direction), edge_zero], axis=direction)
    return take_span(fluxes, 1, cell_count + 1, direction) - take_span(fluxes, 0, cell_count, direction)


def advect_balance(velocity, fraction, velocity_xpad, fraction_xpad):
    along_x = face_balance(velocity_xpad, velocity_xpad[0:1], fraction_xpad, 1, False)
    y_state = jnp.pad(velocity, ((0, 0), (0, 0), (2, 2), (0, 0)), mode="wrap")
    y_fraction = jnp.pad(fraction[None], ((0, 0), (0, 0), (2, 2), (0, 0)), mode="wrap")
    along_y = face_balance(y_state, y_state[1:2], y_fraction, 2, False)
    z_state = jnp.pad(velocity, ((0, 0), (0, 0), (0, 0), (2, 2)), mode="edge")
    z_fraction = jnp.pad(fraction[None], ((0, 0), (0, 0), (0, 0), (2, 2)), mode="edge")
    along_z = face_balance(z_state, z_state[2:3], z_fraction, 3, True)
    return along_x + along_y + along_z


def divergence(x_padded, advanced):
    along_x = x_padded[2:] - x_padded[:-2]
    along_y = jnp.roll(advanced[1], -1, axis=1) - jnp.roll(advanced[1], 1, axis=1)
    z_padded = jnp.pad(advanced[2], ((0, 0), (0, 0), (1, 1)))
    along_z = z_padded[:, :, 2:] - z_padded[:, :, :-2]
    return 0.5 * (along_x + along_y + along_z)


def gradient(x_padded, estimate):
    along_x = 0.5 * (x_padded[2:] - x_padded[:-2])
    along_y = 0.5 * (jnp.roll(estimate, -1, axis=1) - jnp.roll(estimate, 1, axis=1))
    z_padded = jnp.pad(estimate, ((0, 0), (0, 0), (1, 1)), mode="edge")
    along_z = 0.5 * (z_padded[:, :, 2:] - z_padded[:, :, :-2])
    return jnp.stack([along_x, along_y, along_z])


def neighbour_sum(padded):
    middle = padded[1:-1]
    z_padded = jnp.pad(middle, ((0, 0), (0, 0), (1, 1)), mode="edge")
    return (padded[2:] + padded[:-2]) + (jnp.roll(middle, -1, axis=1) + jnp.roll(middle, 1, axis=1)) + (z_padded[:, :, 2:] + z_padded[:, :, :-2])


def relax(middle, neighbours, source, spacing_sq):
    return middle + (damping / 6.0) * (neighbours - 6.0 * middle - spacing_sq * source)


def restrict_field(values):
    x_size, y_size, z_size = values.shape
    return jnp.mean(values.reshape(x_size // 2, 2, y_size // 2, 2, z_size // 2, 2), axis=(1, 3, 5))


def prolong_field(values):
    return jnp.repeat(jnp.repeat(jnp.repeat(values, 2, axis=0), 2, axis=1), 2, axis=2)


def wrap_rim(values):
    return jnp.pad(values, ((1, 1), (0, 0), (0, 0)), mode="wrap")


def smooth_plain(estimate, source, spacing_sq, turns):
    for sweep_index in range(turns):
        estimate = relax(estimate, neighbour_sum(wrap_rim(estimate)), source, spacing_sq)
    return estimate


def vcycle(estimate, source, depth_level):
    spacing_sq = float(4 ** depth_level)
    if depth_level == LEVELS - 1:
        return smooth_plain(estimate, source, spacing_sq, COARSE)
    estimate = smooth_plain(estimate, source, spacing_sq, SWEEPS)
    residue = source - (neighbour_sum(wrap_rim(estimate)) - 6.0 * estimate) / spacing_sq
    coarse_source = restrict_field(residue)
    correction = vcycle(jnp.zeros_like(coarse_source), coarse_source, depth_level + 1)
    estimate = estimate + prolong_field(correction)
    return smooth_plain(estimate, source, spacing_sq, SWEEPS)


def reference(velocity, vfrac_class, cut_cells, cut_count, offsets):
    cell_total = NX * NY * NZ
    fraction = 0.25 * vfrac_class.astype(jnp.float32) + 0.25
    peak_speed = jnp.max(jnp.abs(velocity))
    timestep = courant / (peak_speed + 1e-6)
    velocity_xpad = jnp.pad(velocity, ((0, 0), (2, 2), (0, 0), (0, 0)), mode="wrap")
    fraction_xpad = jnp.pad(fraction[None], ((0, 0), (2, 2), (0, 0), (0, 0)), mode="wrap")
    balance = advect_balance(velocity, fraction, velocity_xpad, fraction_xpad)
    order = jnp.arange(CELLS_CUT, dtype=jnp.int32)
    owner_rank = order // CUT_DEV
    active = (order % CUT_DEV < cut_count[owner_rank]).astype(jnp.float32)
    x_local = cut_cells // (NY * NZ)
    y_index = (cut_cells // NZ) % NY
    z_index = cut_cells % NZ
    x_global = owner_rank * CX + x_local
    x_target = (x_global[None] + offsets // 9 - 1) % NX
    y_target = (y_index[None] + (offsets // 3) % 3 - 1) % NY
    z_target = z_index[None] + offsets % 3 - 1
    hood_sum = jnp.sum(fraction[x_target, y_target, z_target], axis=0)
    cut_flat = (x_global * NY + y_index) * NZ + z_index
    cut_balance = balance.reshape(3, cell_total)[:, cut_flat]
    amount = (-timestep) * cut_balance / hood_sum * active
    spread = jnp.broadcast_to(amount[:, None, :], (3, HOOD, CELLS_CUT)).reshape(3, -1)
    target = ((x_target * NY + y_target) * NZ + z_target).reshape(-1)
    moved = jnp.zeros((3, cell_total), jnp.float32).at[:, target].add(spread)
    cut_mask = jnp.zeros((cell_total,), jnp.float32).at[cut_flat].add(active).reshape(fraction.shape)
    update = -balance / fraction
    advanced = velocity + timestep * update * (1.0 - cut_mask) + moved.reshape(velocity.shape)
    source = divergence(wrap_rim(advanced[0]), advanced)
    potential = jnp.zeros_like(source)
    for cycle_index in range(CYCLES):
        potential = vcycle(potential, source, 0)
    projected = advanced - gradient(wrap_rim(potential), potential)
    return projected, potential
```

```python
import functools

import jax
import jax.numpy as jnp
from jax import lax
from jax.experimental import pallas as pl
from jax.experimental.pallas import tpu as pltpu
from jax.sharding import PartitionSpec as P

MESH = pl.DeviceIdType.MESH
CYCLES = 2
COURANT = 0.5
DAMP = 0.8
WEIGHT = DAMP / 6.0
VH = 3
FH = 2
PAD = 5
SH = 4


def roll(value, shift, axis):
    size = value.shape[axis]
    return pltpu.roll(value, shift % size, axis)


def lanes(shape):
    return lax.broadcasted_iota(jnp.int32, shape, len(shape) - 1)


def minmod(a, b):
    return jnp.maximum(jnp.minimum(a, b), 0.0) + jnp.minimum(jnp.maximum(a, b), 0.0)


def kernel(
    n, vel_hbm, vf_hbm, lists_hbm, proj_ref, pot_ref,
    vp, vfp, lists, mx, frr, mask_ref, bal, amt, moved, rolled, fx, sx, spread_t,
    u_halo, f0, p0a, p0b, land0, f1, p1a, p1b, land1, f2, p2a, p2b, land2, tmp, tmp1,
    bar_send, bar_recv, load_sem, send_sem, recv_sem,
):
    me = lax.axis_index("gx")
    right, left = lax.rem(me + 1, n), lax.rem(me + n - 1, n)
    cx, ny, nz = pot_ref.shape
    shift_z = nz.bit_length() - 1
    slots = lists.shape[2]

    loads = [
        pltpu.make_async_copy(vel_hbm, vp.at[:, VH : VH + cx], load_sem.at[0]),
        pltpu.make_async_copy(vf_hbm, vfp.at[FH : FH + cx], load_sem.at[1]),
        pltpu.make_async_copy(lists_hbm, lists.at[0], load_sem.at[2]),
    ]
    for load in loads:
        load.start()

    barrier = pltpu.get_barrier_semaphore()

    def greet(d, carry):
        pl.semaphore_signal(
            barrier, inc=1, device_id={"gx": lax.rem(me + d, n)}, device_id_type=MESH
        )
        return carry

    lax.fori_loop(1, n, greet, 0)
    pl.semaphore_wait(barrier, n - 1)

    used = [0]

    def send(src, dst, target):
        index = used[0]
        used[0] += 1
        copy = pltpu.make_async_remote_copy(
            src_ref=src, dst_ref=dst, send_sem=send_sem.at[index], recv_sem=recv_sem.at[index],
            device_id={"gx": target}, device_id_type=MESH,
        )
        copy.start()
        return copy

    first = [
        send(vel_hbm.at[:, cx - VH : cx], vp.at[:, 0:VH], right),
        send(vel_hbm.at[:, 0:VH], vp.at[:, VH + cx : VH + cx + VH], left),
        send(vf_hbm.at[cx - FH : cx], vfp.at[0:FH], right),
        send(vf_hbm.at[0:FH], vfp.at[FH + cx : FH + cx + FH], left),
        send(lists_hbm, lists.at[1], right),
        send(lists_hbm, lists.at[2], left),
    ]

    loads[0].wait()

    def peak_step(i, top):
        for q in range(3):
            plane = jnp.abs(vp[q, VH + i])
            top = jnp.maximum(top, plane)
        return top

    top = lax.fori_loop(0, cx, peak_step, jnp.zeros((ny, nz), jnp.float32))
    tile = top[0:8]
    for row in range(8, ny, 8):
        tile = jnp.maximum(tile, top[row : row + 8])
    mx[me] = tile

    def peak_copy(d):
        return pltpu.make_async_remote_copy(
            src_ref=mx.at[me], dst_ref=mx.at[me],
            send_sem=bar_send.at[d], recv_sem=bar_recv.at[d],
            device_id={"gx": lax.rem(me + d, n)}, device_id_type=MESH,
        )

    def peak_send(d, carry):
        peak_copy(d).start()
        return carry

    lax.fori_loop(1, n, peak_send, 0)

    def spread(which):
        held = lists[which]
        cut, count = held[0:1], held[10:11]
        code = lax.shift_left(jnp.ones_like(cut), held[1:2])
        for k in range(2, 10):
            code = code + lax.shift_left(jnp.ones_like(cut), held[k : k + 1])
        live = lax.broadcasted_iota(jnp.int32, cut.shape, 1) < count
        row = jnp.where(live, lax.shift_right_logical(cut, jnp.full_like(cut, shift_z)), -1)
        z_at = jnp.bitwise_and(cut, nz - 1)
        hit = lax.broadcasted_iota(jnp.int32, (nz, slots), 0) == z_at
        for piece in range(4):
            part = jnp.bitwise_and(
                lax.shift_right_logical(code, jnp.full_like(code, 8 * piece)), 255
            ).astype(jnp.float32)
            spread_t[piece * nz : (piece + 1) * nz] = jnp.where(hit, part, 0.0).astype(jnp.bfloat16)
        return row

    def masks(row, begin, rows):
        at = lax.broadcasted_iota(jnp.int32, (rows, slots), 0) + begin
        chosen = jnp.where(at == row, 1.0, 0.0).astype(jnp.bfloat16)
        out = lax.dot_general(
            chosen, spread_t[...], (((1,), (1,)), ((), ())), preferred_element_type=jnp.float32
        )
        total = out[:, 0:nz].astype(jnp.int32)
        for piece in range(1, 4):
            total = total + out[:, piece * nz : (piece + 1) * nz].astype(jnp.int32) * (1 << (8 * piece))
        return total

    loads[2].wait()
    row = spread(0)
    group = 4 if cx % 4 == 0 else 1

    def mask_step(i, carry):
        part = masks(row, i * (group * ny), group * ny)
        for k in range(group):
            mask_ref[1 + i * group + k] = part[k * ny : (k + 1) * ny]
        return carry

    lax.fori_loop(0, cx // group, mask_step, 0)

    def fraction_step(i):
        fraction = 0.25 * vfp[i].astype(jnp.float32) + 0.25
        for dy in range(3):
            base = roll(fraction, 1 - dy, 0)
            for dz in range(3):
                frr[dy * 3 + dz, i] = roll(base, 1 - dz, 1)

    def fraction_body(i, carry):
        fraction_step(i)
        return carry

    loads[1].wait()
    lax.fori_loop(FH, FH + cx, fraction_body, 0)
    for copy in first:
        copy.wait()
    lax.fori_loop(0, FH, fraction_body, 0)
    lax.fori_loop(FH + cx, FH + cx + FH, fraction_body, 0)
    row = spread(1)
    mask_ref[0] = masks(row, (cx - 1) * ny, ny)
    row = spread(2)
    mask_ref[cx + 1] = masks(row, 0, ny)

    def x_slope(q, i):
        here = vp[q, i]
        return minmod(here - vp[q, i - 1], vp[q, i + 1] - here)

    def x_face(i, q_slopes):
        speed = 0.5 * (vp[0, i] + vp[0, i + 1])
        rate = jnp.minimum(frr[4, i - 1], frr[4, i]) * speed
        ahead = speed > 0
        fluxes = []
        for q in range(3):
            below, above = q_slopes[q]
            fluxes.append(
                rate * jnp.where(ahead, vp[q, i] + 0.5 * below, vp[q, i + 1] - 0.5 * above)
            )
        return fluxes

    start = [(x_slope(q, 1), x_slope(q, 2)) for q in range(3)]
    for q, flux in enumerate(x_face(1, start)):
        fx[q] = flux
        sx[q] = start[q][1]

    lane = lanes((ny, nz))

    def balance_step(s, carry):
        i = s + 2
        pairs = [(sx[q], x_slope(q, i + 1)) for q in range(3)]
        upper = x_face(i, pairs)
        fraction = frr[4, i - 1]
        y_speed = 0.5 * (vp[1, i] + roll(vp[1, i], -1, 0))
        y_rate = jnp.minimum(fraction, frr[7, i - 1]) * y_speed
        z_speed = 0.5 * (vp[2, i] + roll(vp[2, i], -1, 1))
        z_rate = jnp.where(lane == nz - 1, 0.0, jnp.minimum(fraction, frr[5, i - 1]) * z_speed)
        inner = jnp.logical_and(lane > 0, lane < nz - 1)
        held = mask_ref[s]
        hood = jnp.zeros((ny, nz), jnp.float32)
        for dx in range(3):
            for k in range(9):
                hood = hood + jnp.where(
                    jnp.bitwise_and(held, 1 << (dx * 9 + k)) != 0, frr[k, i - 2 + dx], 0.0
                )
        scale = 1.0 / jnp.where(held != 0, hood, 1.0)
        for q in range(3):
            value = vp[q, i]
            result = upper[q] - fx[q]
            fx[q] = upper[q]
            sx[q] = pairs[q][1]
            for axis, speed, rate in ((0, y_speed, y_rate), (1, z_speed, z_rate)):
                ahead_value = roll(value, -1, axis)
                slope = minmod(value - roll(value, 1, axis), ahead_value - value)
                if axis == 1:
                    slope = jnp.where(inner, slope, 0.0)
                flux = rate * jnp.where(
                    speed > 0, value + 0.5 * slope, roll(value - 0.5 * slope, -1, axis)
                )
                result = result + (flux - roll(flux, 1, axis))
            bal[q, s] = result
            amt[q, s] = result * scale
        return carry

    lax.fori_loop(0, cx + 2, balance_step, 0)

    def clear(s, carry):
        for q in range(3):
            moved[q, s] = jnp.zeros((ny, nz), jnp.float32)
        return carry

    lax.fori_loop(0, cx + 4, clear, 0)

    def move_step(s, carry):
        for dy in range(3):
            held = roll(mask_ref[s], dy - 1, 0)
            values = [roll(amt[q, s], dy - 1, 0) for q in range(3)]
            for dz in range(3):
                mask_ref[cx + 2 + dy * 3 + dz] = roll(held, dz - 1, 1)
                for q in range(3):
                    rolled[q, dy * 3 + dz] = roll(values[q], dz - 1, 1)
        for dx in range(3):
            sums = [moved[q, s + dx] for q in range(3)]
            for k in range(9):
                chosen = jnp.bitwise_and(mask_ref[cx + 2 + k], 1 << (dx * 9 + k)) != 0
                for q in range(3):
                    sums[q] = sums[q] + jnp.where(chosen, rolled[q, k], 0.0)
            for q in range(3):
                moved[q, s + dx] = sums[q]
        return carry

    lax.fori_loop(0, cx + 2, move_step, 0)

    def peak_wait(d, carry):
        peak_copy(d).wait()
        return carry

    lax.fori_loop(1, n, peak_wait, 0)
    peak = jnp.max(jnp.max(mx[...], axis=0))
    timestep = COURANT / (peak + 1e-06)

    def advance_step(x, carry):
        keep = jnp.where(mask_ref[x + 1] != 0, 0.0, 1.0 / frr[4, x + FH])
        for q in range(3):
            proj_ref[q, x] = vp[q, x + VH] - timestep * (
                bal[q, x + 1] * keep + moved[q, x + 2]
            )
        return carry

    lax.fori_loop(0, cx, advance_step, 0)

    def source_step(x, carry):
        v, w = proj_ref[1, x], proj_ref[2, x]
        w_up = jnp.where(lane == nz - 1, 0.0, roll(w, -1, 1))
        w_down = jnp.where(lane == 0, 0.0, roll(w, 1, 1))
        f0[PAD + x] = 0.5 * ((roll(v, -1, 0) - roll(v, 1, 0)) + (w_up - w_down))
        return carry

    def source_x(x, carry):
        f0[PAD + x] = f0[PAD + x] + 0.5 * (proj_ref[0, x + 1] - proj_ref[0, x - 1])
        return carry

    lax.fori_loop(0, cx, source_step, 0)
    lax.fori_loop(1, cx - 1, source_x, 0)
    f0[PAD] = f0[PAD] + 0.5 * proj_ref[0, 1]
    f0[PAD + cx - 1] = f0[PAD + cx - 1] - 0.5 * proj_ref[0, cx - 2]
    u_halo[0] = proj_ref[0, 0]
    u_halo[1] = proj_ref[0, cx - 1]
    copies = [
        send(f0.at[PAD + cx - SH : PAD + cx], f0.at[PAD - SH : PAD], right),
        send(f0.at[PAD : PAD + SH], f0.at[PAD + cx : PAD + cx + SH], left),
        send(u_halo.at[1], u_halo.at[2], right),
        send(u_halo.at[0], u_halo.at[3], left),
    ]
    for copy in copies:
        copy.wait()
    f0[PAD] = f0[PAD] - 0.5 * u_halo[2]
    f0[PAD + cx - 1] = f0[PAD + cx - 1] + 0.5 * u_halo[3]
    f0[PAD - 1] = f0[PAD - 1] + 0.5 * u_halo[0]
    f0[PAD + cx] = f0[PAD + cx] - 0.5 * u_halo[1]

    chunks = (2, 2, 0)

    def over(level, low, high, body):
        step = chunks[level]
        if step == 0:
            body(PAD + low, high - low)
        else:
            def run(i, carry):
                body(PAD + low + i * step, step)
                return carry
            lax.fori_loop(0, (high - low) // step, run, 0)

    def around(src, at, size, level):
        here = src[pl.ds(at, size)]
        lane_at = lanes(here.shape)
        hop = 1 << level
        z_up = jnp.where(lane_at >= nz - hop, here, roll(here, -hop, 2))
        z_down = jnp.where(lane_at < hop, here, roll(here, hop, 2))
        nbsum = (
            (src[pl.ds(at + 1, size)] + src[pl.ds(at - 1, size)])
            + (roll(here, -1, 1) + roll(here, 1, 1))
            + (z_up + z_down)
        )
        return here, nbsum

    def seed(dst, f, level, low, high):
        def body(at, size):
            dst[pl.ds(at, size)] = (-WEIGHT * 4.0**level) * f[pl.ds(at, size)]
        over(level, low, high, body)

    def sweep(src, dst, f, level, low, high):
        def body(at, size):
            here, nbsum = around(src, at, size, level)
            dst[pl.ds(at, size)] = (1.0 - DAMP) * here + WEIGHT * (
                nbsum - (4.0**level) * f[pl.ds(at, size)]
            )
        over(level, low, high, body)

    def restrict(src, f, coarse, level, low, high, scratch):
        rows = f.shape[1]

        def body(i, carry):
            at = PAD + 2 * (low + i)
            here, nbsum = around(src, at, 2, level)
            residue = f[pl.ds(at, 2)] - (nbsum - 6.0 * here) * (1.0 / 4.0**level)
            scratch[...] = residue[0] + residue[1]
            pair = scratch[pl.ds(0, rows // 2, stride=2), :] + scratch[pl.ds(1, rows // 2, stride=2), :]
            lane_at = lanes(pair.shape)
            hop = 1 << level
            other = jnp.where(
                jnp.bitwise_and(lane_at, hop) == 0, roll(pair, -hop, 1), roll(pair, hop, 1)
            )
            coarse[PAD + low + i] = 0.125 * (pair + other)
            return carry

        lax.fori_loop(0, high - low, body, 0)

    def correct(p, coarse, low, high, scratch):
        rows = p.shape[1]

        def body(i, carry):
            value = coarse[PAD + low + i]
            scratch[pl.ds(0, rows // 2, stride=2), :] = value
            scratch[pl.ds(1, rows // 2, stride=2), :] = value
            at = PAD + 2 * (low + i)
            fine = scratch[...]
            p[at] = p[at] + fine
            p[at + 1] = p[at + 1] + fine
            return carry

        lax.fori_loop(0, high - low, body, 0)

    def planes_in(dst, land, begin, size):
        dst[begin : begin + size] = land[...]

    c1, c2 = cx // 2, cx // 4
    for cycle in range(CYCLES):
        if cycle == 0:
            seed(p0a, f0, 0, -4, cx + 4)
        else:
            copies = [
                send(p0a.at[cx : PAD + cx], land0.at[0], right),
                send(p0a.at[PAD : 2 * PAD], land0.at[1], left),
            ]
            for copy in copies:
                copy.wait()
            planes_in(p0a, land0.at[0], 0, PAD)
            planes_in(p0a, land0.at[1], PAD + cx, PAD)
            sweep(p0a, p0b, f0, 0, -4, cx + 4)
        before, after = (p0a, p0b) if cycle == 0 else (p0b, p0a)
        sweep(before, after, f0, 0, -3, cx + 3)
        restrict(after, f0, f1, 0, 0, c1, tmp)
        copies = [
            send(f1.at[c1 : PAD + c1], land1.at[cycle, 0], right),
            send(f1.at[PAD : 2 * PAD], land1.at[cycle, 1], left),
        ]
        for copy in copies:
            copy.wait()
        planes_in(f1, land1.at[cycle, 0], 0, PAD)
        planes_in(f1, land1.at[cycle, 1], PAD + c1, PAD)
        seed(p1a, f1, 1, -5, c1 + 5)
        sweep(p1a, p1b, f1, 1, -4, c1 + 4)
        restrict(p1b, f1, f2, 1, -1, c2 + 1, tmp1)
        copies = [
            send(f2.at[c2 - 1 + PAD - 4 : PAD + c2], land2.at[cycle, 0], right),
            send(f2.at[PAD : 2 * PAD], land2.at[cycle, 1], left),
        ]
        for copy in copies:
            copy.wait()
        planes_in(f2, land2.at[cycle, 0], 0, PAD)
        planes_in(f2, land2.at[cycle, 1], PAD + c2, PAD)
        seed(p2a, f2, 2, -5, c2 + 5)
        sweep(p2a, p2b, f2, 2, -4, c2 + 4)
        sweep(p2b, p2a, f2, 2, -3, c2 + 3)
        sweep(p2a, p2b, f2, 2, -2, c2 + 2)
        correct(p1b, p2b, -2, c2 + 2, tmp1)
        sweep(p1b, p1a, f1, 1, -3, c1 + 3)
        sweep(p1a, p1b, f1, 1, -2, c1 + 2)
        correct(after, p1b, -2, c1 + 2, tmp)
        sweep(after, before, f0, 0, -2, cx + 2)
        sweep(before, after, f0, 0, -1, cx + 1)
        if cycle == 0:
            p0a, p0b = after, before

    final = after

    def project_step(x, carry):
        here = final[PAD + x]
        pot_ref[x] = here
        proj_ref[0, x] = proj_ref[0, x] - 0.5 * (final[PAD + x + 1] - final[PAD + x - 1])
        proj_ref[1, x] = proj_ref[1, x] - 0.5 * (roll(here, -1, 0) - roll(here, 1, 0))
        z_up = jnp.where(lane == nz - 1, here, roll(here, -1, 1))
        z_down = jnp.where(lane == 0, here, roll(here, 1, 1))
        proj_ref[2, x] = proj_ref[2, x] - 0.5 * (z_up - z_down)
        return carry

    lax.fori_loop(0, cx, project_step, 0)


def local(n, velocity, vfrac_class, cut_cells, cut_count, offsets):
    cx, ny, nz = vfrac_class.shape
    slots = cut_cells.shape[0]
    hood = offsets.shape[0]
    lists = jnp.concatenate(
        [
            cut_cells[None],
            offsets,
            jnp.broadcast_to(cut_count[:, None], (16 - 1 - hood, slots)),
        ]
    )
    f32 = jnp.float32
    vm = pltpu.VMEM
    level = lambda l: vm((cx // 2**l + 2 * PAD, ny // 2**l, nz), f32)
    return tuple(
        pl.pallas_call(
            functools.partial(kernel, n),
            out_shape=(
                jax.ShapeDtypeStruct(velocity.shape, f32),
                jax.ShapeDtypeStruct(vfrac_class.shape, f32),
            ),
            in_specs=[pl.BlockSpec(memory_space=pl.ANY)] * 3,
            out_specs=(pl.BlockSpec(memory_space=pltpu.VMEM),) * 2,
            scratch_shapes=[
                vm((3, cx + 2 * VH, ny, nz), f32),
                vm((cx + 2 * FH, ny, nz), jnp.int32),
                vm((3, 16, slots), jnp.int32),
                vm((n, 8, nz), f32),
                vm((9, cx + 2 * FH, ny, nz), f32),
                vm((cx + 2 + 9, ny, nz), jnp.int32),
                vm((3, cx + 2, ny, nz), f32),
                vm((3, cx + 2, ny, nz), f32),
                vm((3, cx + 4, ny, nz), f32),
                vm((3, 9, ny, nz), f32),
                vm((3, ny, nz), f32),
                vm((3, ny, nz), f32),
                vm((4 * nz, slots), jnp.bfloat16),
                vm((4, ny, nz), f32),
                level(0), level(0), level(0), vm((2, PAD, ny, nz), f32),
                level(1), level(1), level(1), vm((CYCLES, 2, PAD, ny // 2, nz), f32),
                level(2), level(2), level(2), vm((CYCLES, 2, PAD, ny // 4, nz), f32),
                vm((ny, nz), f32),
                vm((ny // 2, nz), f32),
                pltpu.SemaphoreType.DMA((n,)),
                pltpu.SemaphoreType.DMA((n,)),
                pltpu.SemaphoreType.DMA((3,)),
                pltpu.SemaphoreType.DMA((20,)),
                pltpu.SemaphoreType.DMA((20,)),
            ],
            compiler_params=pltpu.CompilerParams(
                collective_id=0, has_side_effects=True, vmem_limit_bytes=48 * 2**20
            ),
        )(velocity, vfrac_class, lists)
    )


def solution(mesh):
    placed = (
        P("grp", "gx", None, None),
        P(("grp", "gx"), None, None),
        P(("grp", "gx")),
        P(("grp", "gx")),
        P("grp", "gx"),
    )
    return jax.shard_map(
        functools.partial(local, mesh.shape["gx"]),
        mesh=mesh,
        in_specs=placed,
        out_specs=(P("grp", "gx", None, None), P(("grp", "gx"), None, None)),
        check_vma=False,
    )
```

```python
import functools

import jax
import jax.numpy as jnp
from jax import lax
from jax.experimental import pallas as pl
from jax.experimental.pallas import tpu as pltpu
from jax.sharding import PartitionSpec as P

MESH = pl.DeviceIdType.MESH
CYCLES = 2
COURANT = 0.5
DAMP = 0.8
WEIGHT = DAMP / 6.0
VH = 3
FH = 2
PAD = 5
SH = 4


def roll(value, shift, axis):
    size = value.shape[axis]
    return pltpu.roll(value, shift % size, axis)


def lanes(shape):
    return lax.broadcasted_iota(jnp.int32, shape, len(shape) - 1)


def planes(low, high, turns, body):
    def run(i, carry):
        for k in range(turns):
            body(low + i * turns + k)
        return carry

    count = (high - low) // turns
    lax.fori_loop(0, count, run, 0)
    for at in range(low + count * turns, high):
        body(at)


def minmod(a, b):
    return jnp.maximum(jnp.minimum(a, b), 0.0) + jnp.minimum(jnp.maximum(a, b), 0.0)


def kernel(
    n, vel_hbm, vf_hbm, lists_hbm, proj_ref, pot_ref,
    vp, vfp, lists, mx, frr, mask_ref, bal, amt, moved, rolled, fx, sx, spread_t,
    u_halo, f0, p0a, p0b, p0c, land0, f1, p1a, p1b, land1, f2, p2a, p2b, land2, tmp, tmp1,
    bar_send, bar_recv, load_sem, send_sem, recv_sem,
):
    me = lax.axis_index("gx")
    right, left = lax.rem(me + 1, n), lax.rem(me + n - 1, n)
    cx, ny, nz = pot_ref.shape
    shift_z = nz.bit_length() - 1
    slots = lists.shape[2]

    loads = [
        pltpu.make_async_copy(vel_hbm, vp.at[:, VH : VH + cx], load_sem.at[0]),
        pltpu.make_async_copy(vf_hbm, vfp.at[FH : FH + cx], load_sem.at[1]),
        pltpu.make_async_copy(lists_hbm, lists.at[0], load_sem.at[2]),
    ]
    for load in loads:
        load.start()

    barrier = pltpu.get_barrier_semaphore()

    def greet(d, carry):
        pl.semaphore_signal(
            barrier, inc=1, device_id={"gx": lax.rem(me + d, n)}, device_id_type=MESH
        )
        return carry

    lax.fori_loop(1, n, greet, 0)
    pl.semaphore_wait(barrier, n - 1)

    used = [0]

    def send(src, dst, target):
        index = used[0]
        used[0] += 1
        copy = pltpu.make_async_remote_copy(
            src_ref=src, dst_ref=dst, send_sem=send_sem.at[index], recv_sem=recv_sem.at[index],
            device_id={"gx": target}, device_id_type=MESH,
        )
        copy.start()
        return copy

    first = [
        send(vel_hbm.at[:, cx - VH : cx], vp.at[:, 0:VH], right),
        send(vel_hbm.at[:, 0:VH], vp.at[:, VH + cx : VH + cx + VH], left),
        send(vf_hbm.at[cx - FH : cx], vfp.at[0:FH], right),
        send(vf_hbm.at[0:FH], vfp.at[FH + cx : FH + cx + FH], left),
        send(lists_hbm, lists.at[1], right),
        send(lists_hbm, lists.at[2], left),
    ]

    loads[0].wait()

    def peak_step(i, top):
        for q in range(3):
            plane = jnp.abs(vp[q, VH + i])
            top = jnp.maximum(top, plane)
        return top

    top = lax.fori_loop(0, cx, peak_step, jnp.zeros((ny, nz), jnp.float32))
    tile = top[0:8]
    for row in range(8, ny, 8):
        tile = jnp.maximum(tile, top[row : row + 8])
    mx[me] = tile

    def peak_copy(d):
        return pltpu.make_async_remote_copy(
            src_ref=mx.at[me], dst_ref=mx.at[me],
            send_sem=bar_send.at[d], recv_sem=bar_recv.at[d],
            device_id={"gx": lax.rem(me + d, n)}, device_id_type=MESH,
        )

    def peak_send(d, carry):
        peak_copy(d).start()
        return carry

    lax.fori_loop(1, n, peak_send, 0)

    def spread(which):
        held = lists[which]
        cut, count = held[0:1], held[10:11]
        code = lax.shift_left(jnp.ones_like(cut), held[1:2])
        for k in range(2, 10):
            code = code + lax.shift_left(jnp.ones_like(cut), held[k : k + 1])
        live = lax.broadcasted_iota(jnp.int32, cut.shape, 1) < count
        row = jnp.where(live, lax.shift_right_logical(cut, jnp.full_like(cut, shift_z)), -1)
        z_at = jnp.bitwise_and(cut, nz - 1)
        hit = lax.broadcasted_iota(jnp.int32, (nz, slots), 0) == z_at
        for piece in range(4):
            part = jnp.bitwise_and(
                lax.shift_right_logical(code, jnp.full_like(code, 8 * piece)), 255
            ).astype(jnp.float32)
            spread_t[piece * nz : (piece + 1) * nz] = jnp.where(hit, part, 0.0).astype(jnp.bfloat16)
        return row

    def masks(row, begin, rows):
        at = lax.broadcasted_iota(jnp.int32, (rows, slots), 0) + begin
        chosen = jnp.where(at == row, 1.0, 0.0).astype(jnp.bfloat16)
        out = lax.dot_general(
            chosen, spread_t[...], (((1,), (1,)), ((), ())), preferred_element_type=jnp.float32
        )
        total = out[:, 0:nz].astype(jnp.int32)
        for piece in range(1, 4):
            total = total + out[:, piece * nz : (piece + 1) * nz].astype(jnp.int32) * (1 << (8 * piece))
        return total

    loads[2].wait()
    row = spread(0)
    group = 4 if cx % 4 == 0 else 1

    def mask_step(i, carry):
        part = masks(row, i * (group * ny), group * ny)
        for k in range(group):
            mask_ref[1 + i * group + k] = part[k * ny : (k + 1) * ny]
        return carry

    lax.fori_loop(0, cx // group, mask_step, 0)

    def fraction_step(i):
        fraction = 0.25 * vfp[i].astype(jnp.float32) + 0.25
        for dy in range(3):
            base = roll(fraction, 1 - dy, 0)
            for dz in range(3):
                frr[dy * 3 + dz, i] = roll(base, 1 - dz, 1)

    loads[1].wait()
    planes(FH, FH + cx, 2, fraction_step)

    def x_slope(q, i):
        here = vp[q, i]
        return minmod(here - vp[q, i - 1], vp[q, i + 1] - here)

    def x_face(i, q_slopes):
        speed = 0.5 * (vp[0, i] + vp[0, i + 1])
        rate = jnp.minimum(frr[4, i - 1], frr[4, i]) * speed
        ahead = speed > 0
        fluxes = []
        for q in range(3):
            below, above = q_slopes[q]
            fluxes.append(
                rate * jnp.where(ahead, vp[q, i] + 0.5 * below, vp[q, i + 1] - 0.5 * above)
            )
        return fluxes

    lane = lanes((ny, nz))

    def balance_step(s, carry):
        i = s + 2
        pairs = [(sx[q], x_slope(q, i + 1)) for q in range(3)]
        upper = x_face(i, pairs)
        fraction = frr[4, i - 1]
        y_speed = 0.5 * (vp[1, i] + roll(vp[1, i], -1, 0))
        y_rate = jnp.minimum(fraction, frr[7, i - 1]) * y_speed
        z_speed = 0.5 * (vp[2, i] + roll(vp[2, i], -1, 1))
        z_rate = jnp.where(lane == nz - 1, 0.0, jnp.minimum(fraction, frr[5, i - 1]) * z_speed)
        inner = jnp.logical_and(lane > 0, lane < nz - 1)
        held = mask_ref[s]
        hood = jnp.zeros((ny, nz), jnp.float32)
        for dx in range(3):
            for k in range(9):
                hood = hood + jnp.where(
                    jnp.bitwise_and(held, 1 << (dx * 9 + k)) != 0, frr[k, i - 2 + dx], 0.0
                )
        scale = 1.0 / jnp.where(held != 0, hood, 1.0)
        for q in range(3):
            value = vp[q, i]
            result = upper[q] - fx[q]
            fx[q] = upper[q]
            sx[q] = pairs[q][1]
            for axis, speed, rate in ((0, y_speed, y_rate), (1, z_speed, z_rate)):
                ahead_value = roll(value, -1, axis)
                slope = minmod(value - roll(value, 1, axis), ahead_value - value)
                if axis == 1:
                    slope = jnp.where(inner, slope, 0.0)
                flux = rate * jnp.where(
                    speed > 0, value + 0.5 * slope, roll(value - 0.5 * slope, -1, axis)
                )
                result = result + (flux - roll(flux, 1, axis))
            bal[q, s] = result
            amt[q, s] = result * scale
        return carry

    def balance_planes(low, high):
        begin = [(x_slope(q, low + 1), x_slope(q, low + 2)) for q in range(3)]
        for q, flux in enumerate(x_face(low + 1, begin)):
            fx[q] = flux
            sx[q] = begin[q][1]
        lax.fori_loop(low, high, balance_step, 0)

    balance_planes(3, cx - 1)
    for copy in first:
        copy.wait()
    planes(0, FH, 2, fraction_step)
    planes(FH + cx, FH + cx + FH, 2, fraction_step)
    row = spread(1)
    mask_ref[0] = masks(row, (cx - 1) * ny, ny)
    row = spread(2)
    mask_ref[cx + 1] = masks(row, 0, ny)
    balance_planes(0, 3)
    balance_planes(cx - 1, cx + 2)

    def clear(s, carry):
        for q in range(3):
            moved[q, s] = jnp.zeros((ny, nz), jnp.float32)
        return carry

    lax.fori_loop(0, cx + 4, clear, 0)

    def move_step(s, carry):
        for dy in range(3):
            held = roll(mask_ref[s], dy - 1, 0)
            values = [roll(amt[q, s], dy - 1, 0) for q in range(3)]
            for dz in range(3):
                mask_ref[cx + 2 + dy * 3 + dz] = roll(held, dz - 1, 1)
                for q in range(3):
                    rolled[q, dy * 3 + dz] = roll(values[q], dz - 1, 1)
        for dx in range(3):
            sums = [moved[q, s + dx] for q in range(3)]
            for k in range(9):
                chosen = jnp.bitwise_and(mask_ref[cx + 2 + k], 1 << (dx * 9 + k)) != 0
                for q in range(3):
                    sums[q] = sums[q] + jnp.where(chosen, rolled[q, k], 0.0)
            for q in range(3):
                moved[q, s + dx] = sums[q]
        return carry

    lax.fori_loop(0, cx + 2, move_step, 0)

    def peak_wait(d, carry):
        peak_copy(d).wait()
        return carry

    lax.fori_loop(1, n, peak_wait, 0)
    peak = jnp.max(jnp.max(mx[...], axis=0))
    timestep = COURANT / (peak + 1e-06)

    def advance_step(x):
        keep = jnp.where(mask_ref[x + 1] != 0, 0.0, 1.0 / frr[4, x + FH])
        for q in range(3):
            proj_ref[q, x] = vp[q, x + VH] - timestep * (
                bal[q, x + 1] * keep + moved[q, x + 2]
            )

    planes(0, cx, 2, advance_step)

    def source_step(x):
        v, w = proj_ref[1, x], proj_ref[2, x]
        w_up = jnp.where(lane == nz - 1, 0.0, roll(w, -1, 1))
        w_down = jnp.where(lane == 0, 0.0, roll(w, 1, 1))
        f0[PAD + x] = 0.5 * ((roll(v, -1, 0) - roll(v, 1, 0)) + (w_up - w_down))

    def source_x(x):
        f0[PAD + x] = f0[PAD + x] + 0.5 * (proj_ref[0, x + 1] - proj_ref[0, x - 1])

    planes(0, cx, 4, source_step)
    planes(1, cx - 1, 7, source_x)
    f0[PAD] = f0[PAD] + 0.5 * proj_ref[0, 1]
    f0[PAD + cx - 1] = f0[PAD + cx - 1] - 0.5 * proj_ref[0, cx - 2]
    u_halo[0] = proj_ref[0, 0]
    u_halo[1] = proj_ref[0, cx - 1]
    copies = [
        send(f0.at[PAD + cx - SH : PAD + cx], f0.at[PAD - SH : PAD], right),
        send(f0.at[PAD : PAD + SH], f0.at[PAD + cx : PAD + cx + SH], left),
        send(u_halo.at[1], u_halo.at[2], right),
        send(u_halo.at[0], u_halo.at[3], left),
    ]

    def finish_source():
        f0[PAD] = f0[PAD] - 0.5 * u_halo[2]
        f0[PAD + cx - 1] = f0[PAD + cx - 1] + 0.5 * u_halo[3]
        f0[PAD - 1] = f0[PAD - 1] + 0.5 * u_halo[0]
        f0[PAD + cx] = f0[PAD + cx] - 0.5 * u_halo[1]

    chunks = (8, 0, 0)

    def over(level, low, high, body):
        step = chunks[level]
        if step == 0:
            body(PAD + low, high - low)
        else:
            def run(i, carry):
                body(PAD + low + i * step, step)
                return carry
            count = (high - low) // step
            lax.fori_loop(0, count, run, 0)
            rest = high - low - count * step
            if rest:
                body(PAD + low + count * step, rest)

    def around(src, at, size, level):
        here = src[pl.ds(at, size)]
        lane_at = lanes(here.shape)
        hop = 1 << level
        z_up = jnp.where(lane_at >= nz - hop, here, roll(here, -hop, 2))
        z_down = jnp.where(lane_at < hop, here, roll(here, hop, 2))
        nbsum = (
            (src[pl.ds(at + 1, size)] + src[pl.ds(at - 1, size)])
            + (roll(here, -1, 1) + roll(here, 1, 1))
            + (z_up + z_down)
        )
        return here, nbsum

    def seed(dst, f, level, low, high):
        def body(at, size):
            dst[pl.ds(at, size)] = (-WEIGHT * 4.0**level) * f[pl.ds(at, size)]
        over(level, low, high, body)

    def sweep(src, dst, f, level, low, high):
        def body(at, size):
            here, nbsum = around(src, at, size, level)
            dst[pl.ds(at, size)] = (1.0 - DAMP) * here + WEIGHT * (
                nbsum - (4.0**level) * f[pl.ds(at, size)]
            )
        over(level, low, high, body)

    def unrolled(count, body, turns):
        def run(i, carry):
            for k in range(turns):
                body(i * turns + k, k)
            return carry

        lax.fori_loop(0, count // turns, run, 0)
        for k in range(count % turns):
            body(count // turns * turns + k, k)

    def restrict(src, f, coarse, level, low, high, scratch):
        rows = f.shape[1]

        def body(i, slot):
            held = scratch.at[slot]
            at = PAD + 2 * (low + i)
            here, nbsum = around(src, at, 2, level)
            residue = f[pl.ds(at, 2)] - (nbsum - 6.0 * here) * (1.0 / 4.0**level)
            held[...] = residue[0] + residue[1]
            pair = held[pl.ds(0, rows // 2, stride=2), :] + held[pl.ds(1, rows // 2, stride=2), :]
            lane_at = lanes(pair.shape)
            hop = 1 << level
            other = jnp.where(
                jnp.bitwise_and(lane_at, hop) == 0, roll(pair, -hop, 1), roll(pair, hop, 1)
            )
            coarse[PAD + low + i] = 0.125 * (pair + other)

        unrolled(high - low, body, scratch.shape[0])

    def correct(p, coarse, low, high, scratch):
        rows = p.shape[1]

        def body(i, slot):
            held = scratch.at[slot]
            value = coarse[PAD + low + i]
            held[pl.ds(0, rows // 2, stride=2), :] = value
            held[pl.ds(1, rows // 2, stride=2), :] = value
            at = PAD + 2 * (low + i)
            fine = held[...]
            p[at] = p[at] + fine
            p[at + 1] = p[at + 1] + fine

        unrolled(high - low, body, scratch.shape[0])

    def planes_in(dst, land, begin, size):
        dst[begin : begin + size] = land[...]

    c1, c2 = cx // 2, cx // 4
    for cycle in range(CYCLES):
        if cycle == 0:
            before, after = p0a, p0b
            seed(before, f0, 0, 1, cx - 1)
        else:
            copies = [
                send(p0a.at[cx : PAD + cx], land0.at[0], right),
                send(p0a.at[PAD : 2 * PAD], land0.at[1], left),
            ]
            before, after = p0b, p0c
            sweep(p0a, before, f0, 0, 1, cx - 1)
        sweep(before, after, f0, 0, 2, cx - 2)
        restrict(after, f0, f1, 0, 2, c1 - 2, tmp)
        for copy in copies:
            copy.wait()
        if cycle == 0:
            finish_source()
            seed(before, f0, 0, -4, 1)
            seed(before, f0, 0, cx - 1, cx + 4)
        else:
            planes_in(p0a, land0.at[0], 0, PAD)
            planes_in(p0a, land0.at[1], PAD + cx, PAD)
            sweep(p0a, before, f0, 0, -4, 1)
            sweep(p0a, before, f0, 0, cx - 1, cx + 4)
        sweep(before, after, f0, 0, -3, 2)
        sweep(before, after, f0, 0, cx - 2, cx + 3)
        restrict(after, f0, f1, 0, 0, 2, tmp)
        restrict(after, f0, f1, 0, c1 - 2, c1, tmp)
        copies = [
            send(f1.at[c1 : PAD + c1], land1.at[cycle, 0], right),
            send(f1.at[PAD : 2 * PAD], land1.at[cycle, 1], left),
        ]
        seed(p1a, f1, 1, 0, c1)
        sweep(p1a, p1b, f1, 1, 1, c1 - 1)
        for copy in copies:
            copy.wait()
        planes_in(f1, land1.at[cycle, 0], 0, PAD)
        planes_in(f1, land1.at[cycle, 1], PAD + c1, PAD)
        seed(p1a, f1, 1, -5, 0)
        seed(p1a, f1, 1, c1, c1 + 5)
        sweep(p1a, p1b, f1, 1, -4, 1)
        sweep(p1a, p1b, f1, 1, c1 - 1, c1 + 4)
        restrict(p1b, f1, f2, 1, -1, c2 + 1, tmp1)
        copies = [
            send(f2.at[c2 - 1 + PAD - 4 : PAD + c2], land2.at[cycle, 0], right),
            send(f2.at[PAD : 2 * PAD], land2.at[cycle, 1], left),
        ]
        for copy in copies:
            copy.wait()
        planes_in(f2, land2.at[cycle, 0], 0, PAD)
        planes_in(f2, land2.at[cycle, 1], PAD + c2, PAD)
        seed(p2a, f2, 2, -5, c2 + 5)
        sweep(p2a, p2b, f2, 2, -4, c2 + 4)
        sweep(p2b, p2a, f2, 2, -3, c2 + 3)
        sweep(p2a, p2b, f2, 2, -2, c2 + 2)
        correct(p1b, p2b, -2, c2 + 2, tmp1)
        sweep(p1b, p1a, f1, 1, -3, c1 + 3)
        sweep(p1a, p1b, f1, 1, -2, c1 + 2)
        correct(after, p1b, -2, c1 + 2, tmp)
        sweep(after, before, f0, 0, -2, cx + 2)
        sweep(before, after, f0, 0, -1, cx + 1)
        if cycle == 0:
            p0a, p0b = after, before

    final = after

    def project_step(x):
        here = final[PAD + x]
        pot_ref[x] = here
        proj_ref[0, x] = proj_ref[0, x] - 0.5 * (final[PAD + x + 1] - final[PAD + x - 1])
        proj_ref[1, x] = proj_ref[1, x] - 0.5 * (roll(here, -1, 0) - roll(here, 1, 0))
        z_up = jnp.where(lane == nz - 1, here, roll(here, -1, 1))
        z_down = jnp.where(lane == 0, here, roll(here, 1, 1))
        proj_ref[2, x] = proj_ref[2, x] - 0.5 * (z_up - z_down)

    planes(0, cx, 4, project_step)


def local(n, velocity, vfrac_class, cut_cells, cut_count, offsets):
    cx, ny, nz = vfrac_class.shape
    slots = cut_cells.shape[0]
    hood = offsets.shape[0]
    lists = jnp.concatenate(
        [
            cut_cells[None],
            offsets,
            jnp.broadcast_to(cut_count[:, None], (16 - 1 - hood, slots)),
        ]
    )
    f32 = jnp.float32
    vm = pltpu.VMEM
    level = lambda l: vm((cx // 2**l + 2 * PAD, ny // 2**l, nz), f32)
    return tuple(
        pl.pallas_call(
            functools.partial(kernel, n),
            out_shape=(
                jax.ShapeDtypeStruct(velocity.shape, f32),
                jax.ShapeDtypeStruct(vfrac_class.shape, f32),
            ),
            in_specs=[pl.BlockSpec(memory_space=pl.ANY)] * 3,
            out_specs=(pl.BlockSpec(memory_space=pltpu.VMEM),) * 2,
            scratch_shapes=[
                vm((3, cx + 2 * VH, ny, nz), f32),
                vm((cx + 2 * FH, ny, nz), jnp.int32),
                vm((3, 16, slots), jnp.int32),
                vm((n, 8, nz), f32),
                vm((9, cx + 2 * FH, ny, nz), f32),
                vm((cx + 2 + 9, ny, nz), jnp.int32),
                vm((3, cx + 2, ny, nz), f32),
                vm((3, cx + 2, ny, nz), f32),
                vm((3, cx + 4, ny, nz), f32),
                vm((3, 9, ny, nz), f32),
                vm((3, ny, nz), f32),
                vm((3, ny, nz), f32),
                vm((4 * nz, slots), jnp.bfloat16),
                vm((4, ny, nz), f32),
                level(0), level(0), level(0), level(0), vm((2, PAD, ny, nz), f32),
                level(1), level(1), level(1), vm((CYCLES, 2, PAD, ny // 2, nz), f32),
                level(2), level(2), level(2), vm((CYCLES, 2, PAD, ny // 4, nz), f32),
                vm((4, ny, nz), f32),
                vm((3, ny // 2, nz), f32),
                pltpu.SemaphoreType.DMA((n,)),
                pltpu.SemaphoreType.DMA((n,)),
                pltpu.SemaphoreType.DMA((3,)),
                pltpu.SemaphoreType.DMA((20,)),
                pltpu.SemaphoreType.DMA((20,)),
            ],
            compiler_params=pltpu.CompilerParams(
                collective_id=0, has_side_effects=True, vmem_limit_bytes=48 * 2**20
            ),
        )(velocity, vfrac_class, lists)
    )


def solution(mesh):
    placed = (
        P("grp", "gx", None, None),
        P(("grp", "gx"), None, None),
        P(("grp", "gx")),
        P(("grp", "gx")),
        P("grp", "gx"),
    )
    return jax.shard_map(
        functools.partial(local, mesh.shape["gx"]),
        mesh=mesh,
        in_specs=placed,
        out_specs=(P("grp", "gx", None, None), P(("grp", "gx"), None, None)),
        check_vma=False,
    )
```

```python
import functools

import jax
import jax.numpy as jnp
from jax import lax
from jax.experimental import pallas as pl
from jax.experimental.pallas import tpu as pltpu
from jax.sharding import PartitionSpec as P

MESH = pl.DeviceIdType.MESH
CYCLES = 2
COURANT = 0.5
DAMP = 0.8
WEIGHT = DAMP / 6.0
VH = 3
FH = 2
PAD = 5
SH = 4


def roll(value, shift, axis):
    size = value.shape[axis]
    return pltpu.roll(value, shift % size, axis)


def lanes(shape):
    return lax.broadcasted_iota(jnp.int32, shape, len(shape) - 1)


def planes(low, high, turns, body):
    def run(i, carry):
        for k in range(turns):
            body(low + i * turns + k)
        return carry

    count = (high - low) // turns
    lax.fori_loop(0, count, run, 0)
    for at in range(low + count * turns, high):
        body(at)


def minmod(a, b):
    return jnp.maximum(jnp.minimum(a, b), 0.0) + jnp.minimum(jnp.maximum(a, b), 0.0)


def kernel(
    n, vel_hbm, vf_hbm, lists_hbm, proj_ref, pot_ref,
    vp, vfp, lists, mx, frr, mask_ref, bal, amt, moved, rolled, fx, sx, spread_t,
    u_halo, f0, p0a, p0b, p0c, land0, f1, p1a, p1b, land1, f2, p2a, p2b, land2, tmp, tmp1,
    bar_send, bar_recv, load_sem, send_sem, recv_sem,
):
    me = lax.axis_index("gx")
    right, left = lax.rem(me + 1, n), lax.rem(me + n - 1, n)
    cx, ny, nz = pot_ref.shape
    shift_z = nz.bit_length() - 1
    slots = lists.shape[2]

    loads = [
        pltpu.make_async_copy(vel_hbm, vp.at[:, VH : VH + cx], load_sem.at[0]),
        pltpu.make_async_copy(vf_hbm, vfp.at[FH : FH + cx], load_sem.at[1]),
        pltpu.make_async_copy(lists_hbm, lists.at[0], load_sem.at[2]),
    ]
    for load in loads:
        load.start()

    barrier = pltpu.get_barrier_semaphore()

    def greet(d, carry):
        pl.semaphore_signal(
            barrier, inc=1, device_id={"gx": lax.rem(me + d, n)}, device_id_type=MESH
        )
        return carry

    lax.fori_loop(1, n, greet, 0)
    pl.semaphore_wait(barrier, n - 1)

    used = [0]

    def send(src, dst, target):
        index = used[0]
        used[0] += 1
        copy = pltpu.make_async_remote_copy(
            src_ref=src, dst_ref=dst, send_sem=send_sem.at[index], recv_sem=recv_sem.at[index],
            device_id={"gx": target}, device_id_type=MESH,
        )
        copy.start()
        return copy

    first = [
        send(vel_hbm.at[:, cx - VH : cx], vp.at[:, 0:VH], right),
        send(vel_hbm.at[:, 0:VH], vp.at[:, VH + cx : VH + cx + VH], left),
        send(vf_hbm.at[cx - FH : cx], vfp.at[0:FH], right),
        send(vf_hbm.at[0:FH], vfp.at[FH + cx : FH + cx + FH], left),
        send(lists_hbm, lists.at[1], right),
        send(lists_hbm, lists.at[2], left),
    ]

    loads[0].wait()

    def peak_step(i, top):
        for q in range(3):
            plane = jnp.abs(vp[q, VH + i])
            top = jnp.maximum(top, plane)
        return top

    top = lax.fori_loop(0, cx, peak_step, jnp.zeros((ny, nz), jnp.float32))
    tile = top[0:8]
    for row in range(8, ny, 8):
        tile = jnp.maximum(tile, top[row : row + 8])
    mx[me] = tile

    def peak_copy(d):
        return pltpu.make_async_remote_copy(
            src_ref=mx.at[me], dst_ref=mx.at[me],
            send_sem=bar_send.at[d], recv_sem=bar_recv.at[d],
            device_id={"gx": lax.rem(me + d, n)}, device_id_type=MESH,
        )

    def peak_send(d, carry):
        peak_copy(d).start()
        return carry

    lax.fori_loop(1, n, peak_send, 0)

    def spread(which):
        held = lists[which]
        cut, count = held[0:1], held[10:11]
        code = lax.shift_left(jnp.ones_like(cut), held[1:2])
        for k in range(2, 10):
            code = code + lax.shift_left(jnp.ones_like(cut), held[k : k + 1])
        live = lax.broadcasted_iota(jnp.int32, cut.shape, 1) < count
        row = jnp.where(live, lax.shift_right_logical(cut, jnp.full_like(cut, shift_z)), -1)
        z_at = jnp.bitwise_and(cut, nz - 1)
        hit = lax.broadcasted_iota(jnp.int32, (nz, slots), 0) == z_at
        for piece in range(4):
            part = jnp.bitwise_and(
                lax.shift_right_logical(code, jnp.full_like(code, 8 * piece)), 255
            ).astype(jnp.float32)
            spread_t[piece * nz : (piece + 1) * nz] = jnp.where(hit, part, 0.0).astype(jnp.bfloat16)
        return row

    def masks(row, begin, rows):
        at = lax.broadcasted_iota(jnp.int32, (rows, slots), 0) + begin
        chosen = jnp.where(at == row, 1.0, 0.0).astype(jnp.bfloat16)
        out = lax.dot_general(
            chosen, spread_t[...], (((1,), (1,)), ((), ())), preferred_element_type=jnp.float32
        )
        total = out[:, 0:nz].astype(jnp.int32)
        for piece in range(1, 4):
            total = total + out[:, piece * nz : (piece + 1) * nz].astype(jnp.int32) * (1 << (8 * piece))
        return total

    loads[2].wait()
    row = spread(0)
    group = 4 if cx % 4 == 0 else 1

    def mask_step(i, carry):
        part = masks(row, i * (group * ny), group * ny)
        for k in range(group):
            mask_ref[1 + i * group + k] = part[k * ny : (k + 1) * ny]
        return carry

    lax.fori_loop(0, cx // group, mask_step, 0)

    def fraction_step(i):
        fraction = 0.25 * vfp[i].astype(jnp.float32) + 0.25
        for dy in range(3):
            base = roll(fraction, 1 - dy, 0)
            for dz in range(3):
                frr[dy * 3 + dz, i] = roll(base, 1 - dz, 1)

    loads[1].wait()
    planes(FH, FH + cx, 2, fraction_step)

    def x_slope(q, i):
        here = vp[q, i]
        return minmod(here - vp[q, i - 1], vp[q, i + 1] - here)

    def x_face(i, q_slopes):
        speed = 0.5 * (vp[0, i] + vp[0, i + 1])
        rate = jnp.minimum(frr[4, i - 1], frr[4, i]) * speed
        ahead = speed > 0
        fluxes = []
        for q in range(3):
            below, above = q_slopes[q]
            fluxes.append(
                rate * jnp.where(ahead, vp[q, i] + 0.5 * below, vp[q, i + 1] - 0.5 * above)
            )
        return fluxes

    lane = lanes((ny, nz))

    def balance_step(s, carry):
        i = s + 2
        pairs = [(sx[q], x_slope(q, i + 1)) for q in range(3)]
        upper = x_face(i, pairs)
        fraction = frr[4, i - 1]
        y_speed = 0.5 * (vp[1, i] + roll(vp[1, i], -1, 0))
        y_rate = jnp.minimum(fraction, frr[7, i - 1]) * y_speed
        z_speed = 0.5 * (vp[2, i] + roll(vp[2, i], -1, 1))
        z_rate = jnp.where(lane == nz - 1, 0.0, jnp.minimum(fraction, frr[5, i - 1]) * z_speed)
        inner = jnp.logical_and(lane > 0, lane < nz - 1)
        held = mask_ref[s]
        hood = jnp.zeros((ny, nz), jnp.float32)
        for dx in range(3):
            for k in range(9):
                hood = hood + jnp.where(
                    jnp.bitwise_and(held, 1 << (dx * 9 + k)) != 0, frr[k, i - 2 + dx], 0.0
                )
        scale = 1.0 / jnp.where(held != 0, hood, 1.0)
        for q in range(3):
            value = vp[q, i]
            result = upper[q] - fx[q]
            fx[q] = upper[q]
            sx[q] = pairs[q][1]
            for axis, speed, rate in ((0, y_speed, y_rate), (1, z_speed, z_rate)):
                ahead_value = roll(value, -1, axis)
                slope = minmod(value - roll(value, 1, axis), ahead_value - value)
                if axis == 1:
                    slope = jnp.where(inner, slope, 0.0)
                flux = rate * jnp.where(
                    speed > 0, value + 0.5 * slope, roll(value - 0.5 * slope, -1, axis)
                )
                result = result + (flux - roll(flux, 1, axis))
            bal[q, s] = result
            amt[q, s] = result * scale
        return carry

    def balance_planes(low, high):
        begin = [(x_slope(q, low + 1), x_slope(q, low + 2)) for q in range(3)]
        for q, flux in enumerate(x_face(low + 1, begin)):
            fx[q] = flux
            sx[q] = begin[q][1]
        lax.fori_loop(low, high, balance_step, 0)

    balance_planes(3, cx - 1)
    for copy in first:
        copy.wait()
    planes(0, FH, 2, fraction_step)
    planes(FH + cx, FH + cx + FH, 2, fraction_step)
    row = spread(1)
    mask_ref[0] = masks(row, (cx - 1) * ny, ny)
    row = spread(2)
    mask_ref[cx + 1] = masks(row, 0, ny)
    balance_planes(0, 3)
    balance_planes(cx - 1, cx + 2)

    def clear(s, carry):
        for q in range(3):
            moved[q, s] = jnp.zeros((ny, nz), jnp.float32)
        return carry

    lax.fori_loop(0, cx + 4, clear, 0)

    def move_step(s, carry):
        for dy in range(3):
            held = roll(mask_ref[s], dy - 1, 0)
            values = [roll(amt[q, s], dy - 1, 0) for q in range(3)]
            for dz in range(3):
                mask_ref[cx + 2 + dy * 3 + dz] = roll(held, dz - 1, 1)
                for q in range(3):
                    rolled[q, dy * 3 + dz] = roll(values[q], dz - 1, 1)
        for dx in range(3):
            sums = [moved[q, s + dx] for q in range(3)]
            for k in range(9):
                chosen = jnp.bitwise_and(mask_ref[cx + 2 + k], 1 << (dx * 9 + k)) != 0
                for q in range(3):
                    sums[q] = sums[q] + jnp.where(chosen, rolled[q, k], 0.0)
            for q in range(3):
                moved[q, s + dx] = sums[q]
        return carry

    lax.fori_loop(0, cx + 2, move_step, 0)

    def peak_wait(d, carry):
        peak_copy(d).wait()
        return carry

    lax.fori_loop(1, n, peak_wait, 0)
    peak = jnp.max(jnp.max(mx[...], axis=0))
    timestep = COURANT / (peak + 1e-06)

    def advance_step(x):
        keep = jnp.where(mask_ref[x + 1] != 0, 0.0, 1.0 / frr[4, x + FH])
        for q in range(3):
            proj_ref[q, x] = vp[q, x + VH] - timestep * (
                bal[q, x + 1] * keep + moved[q, x + 2]
            )

    planes(0, SH + 1, 2, advance_step)
    planes(cx - SH - 1, cx, 2, advance_step)

    def source_step(x):
        v, w = proj_ref[1, x], proj_ref[2, x]
        w_up = jnp.where(lane == nz - 1, 0.0, roll(w, -1, 1))
        w_down = jnp.where(lane == 0, 0.0, roll(w, 1, 1))
        f0[PAD + x] = 0.5 * ((roll(v, -1, 0) - roll(v, 1, 0)) + (w_up - w_down))

    def source_x(x):
        f0[PAD + x] = f0[PAD + x] + 0.5 * (proj_ref[0, x + 1] - proj_ref[0, x - 1])

    planes(0, SH, 4, source_step)
    planes(cx - SH, cx, 4, source_step)
    planes(1, SH, 3, source_x)
    planes(cx - SH, cx - 1, 3, source_x)
    f0[PAD] = f0[PAD] + 0.5 * proj_ref[0, 1]
    f0[PAD + cx - 1] = f0[PAD + cx - 1] - 0.5 * proj_ref[0, cx - 2]
    u_halo[0] = proj_ref[0, 0]
    u_halo[1] = proj_ref[0, cx - 1]
    copies = [
        send(f0.at[PAD + cx - SH : PAD + cx], f0.at[PAD - SH : PAD], right),
        send(f0.at[PAD : PAD + SH], f0.at[PAD + cx : PAD + cx + SH], left),
        send(u_halo.at[1], u_halo.at[2], right),
        send(u_halo.at[0], u_halo.at[3], left),
    ]
    planes(SH + 1, cx - SH - 1, 3, advance_step)
    planes(SH, cx - SH, 4, source_step)
    planes(SH, cx - SH, 4, source_x)

    def finish_source():
        f0[PAD] = f0[PAD] - 0.5 * u_halo[2]
        f0[PAD + cx - 1] = f0[PAD + cx - 1] + 0.5 * u_halo[3]
        f0[PAD - 1] = f0[PAD - 1] + 0.5 * u_halo[0]
        f0[PAD + cx] = f0[PAD + cx] - 0.5 * u_halo[1]

    chunks = (8, 0, 0)

    def over(level, low, high, body):
        step = chunks[level]
        if step == 0:
            body(PAD + low, high - low)
        else:
            def run(i, carry):
                body(PAD + low + i * step, step)
                return carry
            count = (high - low) // step
            lax.fori_loop(0, count, run, 0)
            rest = high - low - count * step
            if rest:
                body(PAD + low + count * step, rest)

    def around(src, at, size, level):
        here = src[pl.ds(at, size)]
        lane_at = lanes(here.shape)
        hop = 1 << level
        z_up = jnp.where(lane_at >= nz - hop, here, roll(here, -hop, 2))
        z_down = jnp.where(lane_at < hop, here, roll(here, hop, 2))
        nbsum = (
            (src[pl.ds(at + 1, size)] + src[pl.ds(at - 1, size)])
            + (roll(here, -1, 1) + roll(here, 1, 1))
            + (z_up + z_down)
        )
        return here, nbsum

    def seed(dst, f, level, low, high):
        def body(at, size):
            dst[pl.ds(at, size)] = (-WEIGHT * 4.0**level) * f[pl.ds(at, size)]
        over(level, low, high, body)

    def sweep(src, dst, f, level, low, high):
        def body(at, size):
            here, nbsum = around(src, at, size, level)
            dst[pl.ds(at, size)] = (1.0 - DAMP) * here + WEIGHT * (
                nbsum - (4.0**level) * f[pl.ds(at, size)]
            )
        over(level, low, high, body)

    def unrolled(count, body, turns):
        def run(i, carry):
            for k in range(turns):
                body(i * turns + k, k)
            return carry

        lax.fori_loop(0, count // turns, run, 0)
        for k in range(count % turns):
            body(count // turns * turns + k, k)

    def restrict(src, f, coarse, level, low, high, scratch):
        rows = f.shape[1]

        def body(i, slot):
            held = scratch.at[slot]
            at = PAD + 2 * (low + i)
            here, nbsum = around(src, at, 2, level)
            residue = f[pl.ds(at, 2)] - (nbsum - 6.0 * here) * (1.0 / 4.0**level)
            held[...] = residue[0] + residue[1]
            pair = held[pl.ds(0, rows // 2, stride=2), :] + held[pl.ds(1, rows // 2, stride=2), :]
            lane_at = lanes(pair.shape)
            hop = 1 << level
            other = jnp.where(
                jnp.bitwise_and(lane_at, hop) == 0, roll(pair, -hop, 1), roll(pair, hop, 1)
            )
            coarse[PAD + low + i] = 0.125 * (pair + other)

        unrolled(high - low, body, scratch.shape[0])

    def correct(p, coarse, low, high, scratch):
        rows = p.shape[1]

        def body(i, slot):
            held = scratch.at[slot]
            value = coarse[PAD + low + i]
            held[pl.ds(0, rows // 2, stride=2), :] = value
            held[pl.ds(1, rows // 2, stride=2), :] = value
            at = PAD + 2 * (low + i)
            fine = held[...]
            p[at] = p[at] + fine
            p[at + 1] = p[at + 1] + fine

        unrolled(high - low, body, scratch.shape[0])

    def planes_in(dst, land, begin, size):
        dst[begin : begin + size] = land[...]

    c1, c2 = cx // 2, cx // 4
    for cycle in range(CYCLES):
        if cycle == 0:
            before, after = p0a, p0b
            seed(before, f0, 0, 1, cx - 1)
        else:
            before, after = p0b, p0c
            sweep(p0a, before, f0, 0, 1, cx - 1)
        sweep(before, after, f0, 0, 2, cx - 2)
        restrict(after, f0, f1, 0, 2, c1 - 2, tmp)
        for copy in copies:
            copy.wait()
        if cycle == 0:
            finish_source()
            seed(before, f0, 0, -4, 1)
            seed(before, f0, 0, cx - 1, cx + 4)
        else:
            planes_in(p0a, land0.at[0], 0, PAD)
            planes_in(p0a, land0.at[1], PAD + cx, PAD)
            sweep(p0a, before, f0, 0, -4, 1)
            sweep(p0a, before, f0, 0, cx - 1, cx + 4)
        sweep(before, after, f0, 0, -3, 2)
        sweep(before, after, f0, 0, cx - 2, cx + 3)
        restrict(after, f0, f1, 0, 0, 2, tmp)
        restrict(after, f0, f1, 0, c1 - 2, c1, tmp)
        copies = [
            send(f1.at[c1 : PAD + c1], land1.at[cycle, 0], right),
            send(f1.at[PAD : 2 * PAD], land1.at[cycle, 1], left),
        ]
        seed(p1a, f1, 1, 0, c1)
        sweep(p1a, p1b, f1, 1, 1, c1 - 1)
        for copy in copies:
            copy.wait()
        planes_in(f1, land1.at[cycle, 0], 0, PAD)
        planes_in(f1, land1.at[cycle, 1], PAD + c1, PAD)
        seed(p1a, f1, 1, -5, 0)
        seed(p1a, f1, 1, c1, c1 + 5)
        sweep(p1a, p1b, f1, 1, -4, 1)
        sweep(p1a, p1b, f1, 1, c1 - 1, c1 + 4)
        restrict(p1b, f1, f2, 1, -1, c2 + 1, tmp1)
        copies = [
            send(f2.at[c2 - 1 + PAD - 4 : PAD + c2], land2.at[cycle, 0], right),
            send(f2.at[PAD : 2 * PAD], land2.at[cycle, 1], left),
        ]
        for copy in copies:
            copy.wait()
        planes_in(f2, land2.at[cycle, 0], 0, PAD)
        planes_in(f2, land2.at[cycle, 1], PAD + c2, PAD)
        seed(p2a, f2, 2, -5, c2 + 5)
        sweep(p2a, p2b, f2, 2, -4, c2 + 4)
        sweep(p2b, p2a, f2, 2, -3, c2 + 3)
        sweep(p2a, p2b, f2, 2, -2, c2 + 2)
        more = 0 if cycle < CYCLES - 1 else 1
        correct(p1b, p2b, -2, c2 + 2, tmp1)
        sweep(p1b, p1a, f1, 1, -2 - more, c1 + 2 + more)
        sweep(p1a, p1b, f1, 1, -1 - more, c1 + 1 + more)
        correct(after, p1b, -1 - more, c1 + 1 + more, tmp)
        sweep(after, before, f0, 0, -1 - more, cx + 1 + more)
        if more:
            sweep(before, after, f0, 0, -1, cx + 1)
        else:
            sweep(before, after, f0, 0, 0, PAD)
            sweep(before, after, f0, 0, cx - PAD, cx)
            copies = [
                send(after.at[cx : PAD + cx], land0.at[0], right),
                send(after.at[PAD : 2 * PAD], land0.at[1], left),
            ]
            sweep(before, after, f0, 0, PAD, cx - PAD)
            p0a, p0b = after, before

    final = after

    def project_step(x):
        here = final[PAD + x]
        pot_ref[x] = here
        proj_ref[0, x] = proj_ref[0, x] - 0.5 * (final[PAD + x + 1] - final[PAD + x - 1])
        proj_ref[1, x] = proj_ref[1, x] - 0.5 * (roll(here, -1, 0) - roll(here, 1, 0))
        z_up = jnp.where(lane == nz - 1, here, roll(here, -1, 1))
        z_down = jnp.where(lane == 0, here, roll(here, 1, 1))
        proj_ref[2, x] = proj_ref[2, x] - 0.5 * (z_up - z_down)

    planes(0, cx, 4, project_step)


def local(n, velocity, vfrac_class, cut_cells, cut_count, offsets):
    cx, ny, nz = vfrac_class.shape
    slots = cut_cells.shape[0]
    hood = offsets.shape[0]
    lists = jnp.concatenate(
        [
            cut_cells[None],
            offsets,
            jnp.broadcast_to(cut_count[:, None], (16 - 1 - hood, slots)),
        ]
    )
    f32 = jnp.float32
    vm = pltpu.VMEM
    level = lambda l: vm((cx // 2**l + 2 * PAD, ny // 2**l, nz), f32)
    return tuple(
        pl.pallas_call(
            functools.partial(kernel, n),
            out_shape=(
                jax.ShapeDtypeStruct(velocity.shape, f32),
                jax.ShapeDtypeStruct(vfrac_class.shape, f32),
            ),
            in_specs=[pl.BlockSpec(memory_space=pl.ANY)] * 3,
            out_specs=(pl.BlockSpec(memory_space=pltpu.VMEM),) * 2,
            scratch_shapes=[
                vm((3, cx + 2 * VH, ny, nz), f32),
                vm((cx + 2 * FH, ny, nz), jnp.int32),
                vm((3, 16, slots), jnp.int32),
                vm((n, 8, nz), f32),
                vm((9, cx + 2 * FH, ny, nz), f32),
                vm((cx + 2 + 9, ny, nz), jnp.int32),
                vm((3, cx + 2, ny, nz), f32),
                vm((3, cx + 2, ny, nz), f32),
                vm((3, cx + 4, ny, nz), f32),
                vm((3, 9, ny, nz), f32),
                vm((3, ny, nz), f32),
                vm((3, ny, nz), f32),
                vm((4 * nz, slots), jnp.bfloat16),
                vm((4, ny, nz), f32),
                level(0), level(0), level(0), level(0), vm((2, PAD, ny, nz), f32),
                level(1), level(1), level(1), vm((CYCLES, 2, PAD, ny // 2, nz), f32),
                level(2), level(2), level(2), vm((CYCLES, 2, PAD, ny // 4, nz), f32),
                vm((4, ny, nz), f32),
                vm((3, ny // 2, nz), f32),
                pltpu.SemaphoreType.DMA((n,)),
                pltpu.SemaphoreType.DMA((n,)),
                pltpu.SemaphoreType.DMA((3,)),
                pltpu.SemaphoreType.DMA((20,)),
                pltpu.SemaphoreType.DMA((20,)),
            ],
            compiler_params=pltpu.CompilerParams(
                collective_id=0, has_side_effects=True, vmem_limit_bytes=48 * 2**20
            ),
        )(velocity, vfrac_class, lists)
    )


def solution(mesh):
    placed = (
        P("grp", "gx", None, None),
        P(("grp", "gx"), None, None),
        P(("grp", "gx")),
        P(("grp", "gx")),
        P("grp", "gx"),
    )
    return jax.shard_map(
        functools.partial(local, mesh.shape["gx"]),
        mesh=mesh,
        in_specs=placed,
        out_specs=(P("grp", "gx", None, None), P(("grp", "gx"), None, None)),
        check_vma=False,
    )
```
